32 devices in a mesh: row: 2 (over y), col: 4 (over x, core), depth: 4 (over z).
Axes of the slice: x: 2, y: 2, z: 4, core: 2. Of those that a mesh axis runs over, the one named last changes fastest.
Arguments:
- tokens: bfloat16 [2048, 5120], P(('row', 'depth'), 'col'), may hold values from -6 to 6
- w_up: bfloat16 [5120, 20480], P('col', ('row', 'depth')), may hold values from -0.078125 to 0.078125
- bias_up: float32 [20480], P(('row', 'depth')), may hold values from -3 to 3
- w_down: bfloat16 [20480, 5120], P(('row', 'depth'), 'col'), may hold values from -0.0390625 to 0.0390625
- cotangent: bfloat16 [2048, 5120], P(('row', 'depth'), 'col'), may hold values from -6 to 6
Outputs:
- input_grad: bfloat16 [2048, 5120], P(('row', 'depth'), 'col')
- up_grad: float32 [5120, 20480], P('col', ('row', 'depth'))
- up_bias_grad: float32 [20480], P(('row', 'depth'))
- down_grad: float32 [20480, 5120], P(('row', 'depth'), 'col')
- down_bias_grad: float32 [5120], P('col')
The draws below stay inside these ranges and needn't reach their ends.
All inputs are finite; a program needn't handle non-finite values.
Results may differ from the reference program's by a relative error of at most 0.005.
Values may be sent and summed in bfloat16 or wider, within the bound.
A program may use at most 256 MiB of HBM per device.

```python
import jax
import jax.numpy as jnp
from jax import lax

D = 5120
FF = 20480
TOKENS = 2048


def block_scale(rng, shape, cuts, smallest, largest):
    gain = 1.0
    for position, blocks in cuts:
        steps = jax.random.uniform(jax.random.fold_in(jax.random.fold_in(rng, 6), position), (blocks,), jnp.float32, smallest / len(cuts), largest / len(cuts))
        gain = gain * jnp.repeat(jnp.exp(steps), shape[position] // blocks).reshape((-1,) + (1,) * (len(shape) - 1 - position))
    return gain


def centred(key, shape, scale, bound, split=(), dtype=jnp.bfloat16):
    result = jax.random.normal(key, shape, jnp.float32) * scale
    if len(split) > 0:
        result = block_scale(key, shape, split, -0.22, 0.18) * result
    return jnp.clip(result, min=-bound, max=bound).astype(dtype)


def setup_inputs(seed: int = 0) -> dict:
    arg_keys = jax.random.split(jax.random.key(seed), 6)
    tokens = centred(arg_keys[0], (TOKENS, D), 1.0, 6.0, ((0, 8), (1, 4)))
    w_up = centred(arg_keys[1], (D, FF), D ** -0.5, 0.078125, ((0, 4), (1, 8)))
    bias_up = centred(arg_keys[2], (FF,), 0.5, 3.0, ((0, 8),), jnp.float32)
    w_down = centred(arg_keys[3], (FF, D), FF ** -0.5, 0.0390625, ((0, 8), (1, 4)))
    cotangent = centred(arg_keys[4], (TOKENS, D), 1.0, 6.0, ((0, 8), (1, 4)))
    return dict(tokens=tokens, w_up=w_up, bias_up=bias_up, w_down=w_down, cotangent=cotangent)


def gelu_pair(preact):
    normal_cdf = 0.5 * (1.0 + lax.erf(preact * 0.7071067811865476))
    normal_pdf = jnp.exp(-0.5 * preact * preact) * 0.3989422804014327
    return preact * normal_cdf, normal_cdf + preact * normal_pdf


def reference(tokens, w_up, bias_up, w_down, cotangent):
    preact = jnp.dot(tokens, w_up, preferred_element_type=jnp.float32) + bias_up
    activated, derivative = gelu_pair(preact)
    activated = activated.astype(jnp.bfloat16)
    back = jnp.dot(cotangent, w_down.T, preferred_element_type=jnp.float32)
    grad_hidden = (back * derivative).astype(jnp.bfloat16)
    down_grad = jnp.dot(activated.T, cotangent, preferred_element_type=jnp.float32)
    up_grad = jnp.dot(tokens.T, grad_hidden, preferred_element_type=jnp.float32)
    up_bias_grad = jnp.sum(grad_hidden.astype(jnp.float32), axis=0)
    down_bias_grad = jnp.sum(cotangent.astype(jnp.float32), axis=0)
    input_grad = jnp.dot(grad_hidden, w_up.T, preferred_element_type=jnp.float32).astype(jnp.bfloat16)
    return input_grad, up_grad, up_bias_grad, down_grad, down_bias_grad
```

```python
import jax
import jax.numpy as jnp
from jax import lax
from jax.sharding import PartitionSpec as P

CHUNKS = ("own", 0, 1, 2, 3)
PIECES = 4
GROUPS = ((0, 1, 2), (3, 4))


def gelu_pair(preact):
    normal_cdf = 0.5 * (1.0 + lax.erf(preact * 0.7071067811865476))
    normal_pdf = jnp.exp(-0.5 * preact * preact) * 0.3989422804014327
    return (preact * normal_cdf, normal_cdf + preact * normal_pdf)


def times_transpose(left_rows, matrix):
    return lax.dot_general(
        left_rows, matrix, (((1,), (1,)), ((), ())), preferred_element_type=jnp.float32
    )


def over_tokens(left_rows, right_rows):
    return lax.dot_general(
        left_rows, right_rows, (((0,), (0,)), ((), ())), preferred_element_type=jnp.float32
    )


def swap(array, bit, axis="col"):
    pairs = [(i, i ^ bit) for i in range(lax.axis_size(axis))]
    return lax.ppermute(array, axis, pairs)


def steps():
    return [
        (1 << k, axis) for axis in ("depth", "row") for k in range(lax.axis_size(axis).bit_length() - 1)
    ]


def quarter(array, index):
    rows = array.shape[0] // 4
    return lax.dynamic_slice_in_dim(array, index * rows, rows, 0)


def after(array, *earlier):
    return lax.optimization_barrier((array, earlier))[0]


def over_cores(partial):
    half = partial.shape[0] // 2
    return partial[:half] + swap(partial[half:].astype(jnp.bfloat16), 1).astype(jnp.float32)


def over_chips(partial):
    half = partial.shape[0] // 2
    return partial[:half] + swap(partial[half:].astype(jnp.bfloat16), 2).astype(jnp.float32)


def spread(mine):
    both = jnp.concatenate([mine, swap(mine, 2)], axis=0)
    return jnp.concatenate([both, swap(both, 1)], axis=0)


def gather_others(block):
    exchanges = steps()
    for bit, axis in exchanges[:-1]:
        block = jnp.concatenate([block, swap(block, bit, axis)], axis=2)
    return jnp.concatenate([block[:, :, 1:], swap(block, *exchanges[-1])], axis=2), block


def scatter_others(part):
    total = None
    for bit, axis in reversed(steps()):
        if total is None:
            half = (part.shape[1] + 1) // 2
            got = swap(part[:, half - 1 :].astype(jnp.bfloat16), bit, axis).astype(jnp.float32)
            total = jnp.concatenate([got[:, :1], got[:, 1:] + part[:, : half - 1]], axis=1)
        else:
            half = total.shape[1] // 2
            kind = jnp.bfloat16 if half > 1 else jnp.float32
            total = total[:, :half] + swap(total[:, half:].astype(kind), bit, axis).astype(jnp.float32)
    return total


def body(tokens, w_up, bias_up, w_down, cotangent):
    me = lax.axis_index("col")
    rows, width = tokens.shape
    order = (0, 2, 1, 3)
    fourth = rows // 4

    def relative(array):
        return jnp.stack([quarter(array, me ^ j) for j in order])

    local = jnp.stack([relative(tokens), relative(cotangent)])
    last = len(CHUNKS) - 1
    stacked, blocks, gathered = [], [], None
    for chunk in CHUNKS:
        if chunk == "own":
            stacked.append(local)
        else:
            piece = slice(fourth * chunk // PIECES, fourth * (chunk + 1) // PIECES)
            block = local[:, :, None, piece]
            if gathered is not None:
                block = after(block, gathered)
            whole, gathered = gather_others(block)
            stacked.append(whole)

    token_parts, cotan_parts, sums, pairs, hidden_parts, activated_parts, grads = [], [], [], [], [], [], []
    input_own, input_others = None, []

    def forward(i):
        both = stacked[i].reshape(2, -1, width)
        if i >= 1:
            both = after(both, *sums[i - 1])
        if i >= 2:
            both = after(both, *pairs[i - 2])
        if i >= 3:
            both = after(both, hidden_parts[i - 3], activated_parts[i - 3])
        token_rows, cotan_rows = both
        token_parts.append(token_rows)
        cotan_parts.append(cotan_rows)
        preact = over_cores(jnp.dot(token_rows, w_up, preferred_element_type=jnp.float32))
        back = over_cores(times_transpose(cotan_rows, w_down))
        sums.append((preact, back))

    def middle(i):
        preact, back = (over_chips(partial) for partial in sums[i])
        if i == last:
            preact = after(preact, *grads[0])
        activated, derivative = gelu_pair(preact + bias_up)
        pairs.append((activated.astype(jnp.bfloat16), (back * derivative).astype(jnp.bfloat16)))

    def backward(i):
        nonlocal input_own
        activated, hidden = pairs[i]
        hidden_parts.append(spread(hidden))
        activated_parts.append(spread(activated))
        part = times_transpose(hidden_parts[i], w_up)
        if CHUNKS[i] == "own":
            input_own = part.reshape(4, fourth, width)
        else:
            part = part.reshape(stacked[i].shape[1:])
            input_others.append(scatter_others(part).reshape(4, -1, width))
        for group in GROUPS:
            if i == group[-1]:
                token_rows, cotan_rows, hidden_rows, activated_rows = (
                    jnp.concatenate([parts[i] for i in group], axis=0)
                    for parts in (token_parts, cotan_parts, hidden_parts, activated_parts)
                )
                grads.append(
                    (
                        over_tokens(token_rows, hidden_rows),
                        jnp.sum(hidden_rows, axis=0, dtype=jnp.float32),
                        over_tokens(activated_rows, cotan_rows),
                        jnp.sum(cotan_rows, axis=0, dtype=jnp.float32),
                    )
                )

    for i in range(last + 3):
        if i <= last:
            forward(i)
        if 1 <= i <= last + 1:
            middle(i - 1)
        if i >= 2:
            backward(i - 2)
    up_grad, up_bias_grad, down_grad, down_bias_grad = (sum(parts) for parts in zip(*grads))
    input_grad = (input_own + jnp.concatenate(input_others, axis=1)).astype(jnp.bfloat16)
    input_grad = input_grad.reshape(rows, width)
    input_grad = jnp.concatenate(
        [quarter(input_grad, (2 * (j & 1)) | (j >> 1)) for j in [me ^ q for q in range(4)]], axis=0
    )
    return (input_grad, up_grad, up_bias_grad, down_grad, down_bias_grad)


def solution(mesh):
    return jax.shard_map(
        body,
        mesh=mesh,
        in_specs=(
            P(("row", "depth"), "col"),
            P("col", ("row", "depth")),
            P(("row", "depth")),
            P(("row", "depth"), "col"),
            P(("row", "depth"), "col"),
        ),
        out_specs=(
            P(("row", "depth"), "col"),
            P("col", ("row", "depth")),
            P(("row", "depth")),
            P(("row", "depth"), "col"),
            P("col"),
        ),
        check_vma=False,
    )
```

```python
import jax
import jax.numpy as jnp
from jax import lax
from jax.sharding import PartitionSpec as P

CHUNKS = (None, (0, 2), (2, 4), (4, 6), (6, 8))
GROUPS = ((0, 1, 2), (3, 4))


def gelu_pair(preact):
    normal_cdf = 0.5 * (1.0 + lax.erf(preact * 0.7071067811865476))
    normal_pdf = jnp.exp(-0.5 * preact * preact) * 0.3989422804014327
    return (preact * normal_cdf, normal_cdf + preact * normal_pdf)


def times_transpose(left_rows, matrix):
    return lax.dot_general(
        left_rows, matrix, (((1,), (1,)), ((), ())), preferred_element_type=jnp.float32
    )


def over_tokens(left_rows, right_rows):
    return lax.dot_general(
        left_rows, right_rows, (((0,), (0,)), ((), ())), preferred_element_type=jnp.float32
    )


def swap(array, bit, axis="col"):
    pairs = [(i, i ^ bit) for i in range(lax.axis_size(axis))]
    return lax.ppermute(array, axis, pairs)


def steps():
    return [
        (1 << k, axis) for axis in ("depth", "row") for k in range(lax.axis_size(axis).bit_length() - 1)
    ]


def quarter(array, index):
    rows = array.shape[0] // 4
    return lax.dynamic_slice_in_dim(array, index * rows, rows, 0)


def body(tokens, w_up, bias_up, w_down, cotangent):
    me = lax.axis_index("col")
    rows, width = tokens.shape
    fourth = rows // 4
    exchanges = steps()
    last_step = len(exchanges) - 1
    last = len(CHUNKS) - 1

    def relative(array):
        return jnp.stack([quarter(array, me ^ j) for j in (0, 2, 1, 3)])

    def joined(*arrays, axis=0):
        return jnp.concatenate(arrays, axis=axis)

    state = {"local": jnp.stack([relative(tokens), relative(cotangent)]), "weights": (w_up, w_down)}

    def gather(i, first, final):
        for step in range(first, final + 1):
            if step == 0:
                low, high = CHUNKS[i]
                block = state["local"][:, :, None, fourth * low // 8 : fourth * high // 8]
            else:
                block = joined(*state["gather", i], axis=2)
            state["gather", i] = (block, swap(block, *exchanges[step]))

    def z1(i):
        gather(i, 0, 0)

    def z2(i):
        gather(i, 1, last_step - 1)

    def y(i):
        gather(i, last_step, last_step)

    def forward(i):
        if CHUNKS[i] is None:
            stacked = state["local"]
        else:
            block, got = state.pop(("gather", i))
            stacked = joined(block[:, :, 1:], got, axis=2)
        token_rows, cotan_rows = stacked.reshape(2, -1, width)
        state["rows", i] = (token_rows, cotan_rows)
        up, down = state["weights"]
        half = token_rows.shape[0] // 2
        state["sums", i] = tuple(
            (part[:half], part[half:].astype(jnp.bfloat16))
            for part in (
                jnp.dot(token_rows, up, preferred_element_type=jnp.float32),
                times_transpose(cotan_rows, down),
            )
        )

    def over_cores(i):
        state["sums", i] = tuple((mine, swap(send, 1)) for mine, send in state["sums", i])

    def over_chips(i):
        pairs = []
        for mine, got in state["sums", i]:
            total = mine + got.astype(jnp.float32)
            half = total.shape[0] // 2
            pairs.append((total[:half], swap(total[half:].astype(jnp.bfloat16), 2)))
        state["sums", i] = tuple(pairs)

    def spread_chips(i):
        preact, back = (mine + got.astype(jnp.float32) for mine, got in state.pop(("sums", i)))
        value, derivative = gelu_pair(preact + bias_up)
        pair = ((back * derivative).astype(jnp.bfloat16), value.astype(jnp.bfloat16))
        state["pair", i] = tuple((part, swap(part, 2)) for part in pair)

    def spread_cores(i):
        halves = [joined(*pair) for pair in state["pair", i]]
        state["pair", i] = tuple((half, swap(half, 1)) for half in halves)

    def backward(i):
        hidden, activated = (joined(*pair) for pair in state.pop(("pair", i)))
        state["hidden", i], state["activated", i] = hidden, activated
        part = times_transpose(hidden, state["weights"][0])
        if CHUNKS[i] is None:
            state["total", i] = part.reshape(4, fourth, width)
        else:
            low, high = CHUNKS[i]
            part = part.reshape(4, -1, fourth * high // 8 - fourth * low // 8, width)
            half = (part.shape[1] + 1) // 2
            state["part", i] = (part[:, : half - 1], part[:, half - 1 :].astype(jnp.bfloat16))

    def ry(i):
        keep, send = state["part", i]
        state["part", i] = (keep, swap(send, *exchanges[last_step]))

    def scatter(i, step):
        keep, got = state["part", i]
        got = got.astype(jnp.float32)
        if step == last_step - 1:
            total = joined(got[:, :1], got[:, 1:] + keep, axis=1)
        else:
            total = keep + got
        half = total.shape[1] // 2
        kind = jnp.bfloat16 if half > 1 else jnp.float32
        state["part", i] = (total[:, :half], swap(total[:, half:].astype(kind), *exchanges[step]))

    def rz2(i):
        for step in range(last_step - 1, 0, -1):
            scatter(i, step)

    def rz1(i):
        scatter(i, 0)

    def weight_grad(name, other, which, flip):
        left, right = (
            joined(*(state[key, i][k] if key == "rows" else state[key, i] for i in GROUPS[which]))
            for key, k in ((("rows", 0), (other, None)) if not flip else ((other, None), ("rows", 1)))
        )
        grad = over_tokens(left, right), jnp.sum(right, axis=0, dtype=jnp.float32)
        if which > 0:
            grad = tuple(new + old for new, old in zip(grad, state[name]))
        state[name] = grad

    def up(which):
        weight_grad("up", "hidden", which, False)

    def down(which):
        weight_grad("down", "activated", which, True)

    phases = (
        ((forward, 0), (over_cores, 0), (z1, 1)),
        ((over_chips, 0), (z2, 1), (z1, 2)),
        ((spread_chips, 0), (y, 1), (z2, 2)),
        ((forward, 1), (over_cores, 1), (spread_cores, 0), (y, 2), (z1, 3)),
        ((over_chips, 1), (forward, 2), (z2, 3), (backward, 0)),
        ((spread_chips, 1), (over_cores, 2), (y, 3), (z1, 4)),
        ((over_chips, 2), (forward, 3), (z2, 4), (spread_cores, 1)),
        ((spread_chips, 2), (over_cores, 3), (y, 4)),
        ((over_chips, 3), (forward, 4), (spread_cores, 2), (backward, 1)),
        ((spread_chips, 3), (over_cores, 4), (ry, 1)),
        ((over_chips, 4), (spread_cores, 3), (backward, 2), (rz2, 1), (up, 0)),
        ((spread_chips, 4), (backward, 3), (ry, 2), (rz1, 1), (down, 0)),
        ((spread_cores, 4), (backward, 4), (ry, 3), (rz2, 2)),
        ((ry, 4), (rz2, 3), (rz1, 2), (up, 1)),
        ((rz2, 4), (rz1, 3), (down, 1)),
        ((rz1, 4),),
    )
    for phase in phases:
        for work, i in phase:
            work(i)
        keys = list(state)
        values = lax.optimization_barrier(tuple(state[key] for key in keys))
        state = dict(zip(keys, values))

    (up_grad, up_bias_grad), (down_grad, down_bias_grad) = state["up"], state["down"]
    others = [sum(state["part", i]).reshape(4, -1, width) for i in range(1, last + 1)]
    input_grad = (state["total", 0] + joined(*others, axis=1)).astype(jnp.bfloat16)
    input_grad = input_grad.reshape(rows, width)
    input_grad = joined(*(quarter(input_grad, (2 * (j & 1)) | (j >> 1)) for j in [me ^ q for q in range(4)]))
    return (input_grad, up_grad, up_bias_grad, down_grad, down_bias_grad)


def solution(mesh):
    return jax.shard_map(
        body,
        mesh=mesh,
        in_specs=(
            P(("row", "depth"), "col"),
            P("col", ("row", "depth")),
            P(("row", "depth")),
            P(("row", "depth"), "col"),
            P(("row", "depth"), "col"),
        ),
        out_specs=(
            P(("row", "depth"), "col"),
            P("col", ("row", "depth")),
            P(("row", "depth")),
            P(("row", "depth"), "col"),
            P("col"),
        ),
        check_vma=False,
    )
```
